32 devices in a mesh: tok: 16 (over z, y, core), col: 2 (over x).
Axes of the slice: x: 2, y: 2, z: 4, core: 2. Of those that a mesh axis runs over, the one named last changes fastest.
Arguments:
- activations: bfloat16 [16384, 4096], P('tok'), may hold values from -14 to 14
- targets: bfloat16 [16384, 4096], P('tok', 'col'), may hold values from -20 to 20
- map_weight: float32 [4096, 4096], P('tok', 'col'), may hold values from -1 to 2
- first_moment: float32 [4096, 4096], P('tok', 'col'), may hold values from -0.12 to 0.12
- second_moment: float32 [4096, 4096], P('tok', 'col'), may hold values from 0.0001 to 0.001
- down_weight: bfloat16 [14336, 4096], P('tok', 'col'), may hold values from -6 to 6
Outputs:
- new_map: float32 [4096, 4096], P('tok', 'col')
- joined: bfloat16 [14336, 4096], P('tok', 'col')
The draws below stay inside these ranges and needn't reach their ends.
All inputs are finite; a program needn't handle non-finite values.
Results may differ from the reference program's by a relative error of at most 0.0041.
The reference program's roundings to bfloat16 on the way (of `map_half` and `d_pred`) count: a program that leaves them out, or rounds other values in their place, can miss the bound.
Values may be sent and summed in bfloat16 or wider, within the bound.
A program may use at most 128 MiB of HBM per device.

```python
import math
import jax
import jax.numpy as jnp
from jax import lax

D = 4096
FF = 14336
TOKENS = 16384


def token_fields(key):
    base_key = jax.random.fold_in(key, 7)
    noise_key = jax.random.fold_in(key, 11)
    base = jax.random.truncated_normal(base_key, -4.0, 4.0, (TOKENS, D), jnp.float32)
    noise = jax.random.truncated_normal(noise_key, -4.0, 4.0, (TOKENS, D), jnp.float32)
    inputs = base
    outputs = 0.7 * base + 0.7 * noise
    return (inputs, outputs)


def draw_activations(key, part):
    inputs, outputs = token_fields(key)
    return inputs.astype(jnp.bfloat16)


def draw_targets(key, part):
    inputs, outputs = token_fields(key)
    return outputs.astype(jnp.bfloat16)


def draw_map_weight(key, part):
    noise_key = jax.random.fold_in(key, 23)
    spread = 1.0 / jnp.sqrt(jnp.float32(D))
    noise = jax.random.truncated_normal(noise_key, -4.0, 4.0, (D, D), jnp.float32) * spread
    return (jnp.eye(D, dtype=jnp.float32) + noise).astype(jnp.float32)


def shard_levels(key, dims, pieces, least, largest):
    factor_of, own = 1.0, jax.random.fold_in(key, 6)
    for position, shards_of in pieces:
        draws = jnp.exp(jax.random.uniform(jax.random.fold_in(own, position), (shards_of,), jnp.float32, least / len(pieces), largest / len(pieces)))
        factor_of = factor_of * jnp.repeat(draws, dims[position] // shards_of).reshape([-1 if axis == position else 1 for axis in range(len(dims))])
    return factor_of


def normal_values(own_key, extent, deviation, most, split=(), kind=jnp.bfloat16):
    drawn = deviation * jax.random.normal(own_key, extent, jnp.float32)
    if split:
        drawn = drawn * shard_levels(own_key, extent, split, -0.22, 0.18)
    return jnp.clip(drawn, -most, most).astype(kind)


def setup_inputs(seed: int = 0) -> dict:
    keys = jax.random.split(jax.random.key(seed), 7)
    return {
        "activations": draw_activations(jax.random.fold_in(keys[6], 71), 0),
        "targets": draw_targets(jax.random.fold_in(keys[6], 71), 0),
        "map_weight": draw_map_weight(jax.random.fold_in(keys[6], 71), 0),
        "first_moment": normal_values(keys[3], (D, D), 0.02, 0.12, ((0, 16), (1, 2)), jnp.float32),
        "second_moment": jnp.clip(jnp.exp(math.log(0.001) - 2.3025852 * jax.random.uniform(keys[4], (D, D), jnp.float32) ** shard_levels(keys[4], (D, D), ((0, 16), (1, 2)), -0.2, 0.2)), 0.0001, 0.001),
        "down_weight": normal_values(keys[5], (FF, D), 1.0, 6.0, ((0, 16), (1, 2))),
    }


def reference(activations, targets, map_weight, first_moment, second_moment, down_weight):
    high = lax.Precision.HIGHEST
    map_half = map_weight.astype(jnp.bfloat16)
    inputs = activations.astype(jnp.float32)
    predicted = jnp.dot(inputs, map_half.astype(jnp.float32), precision=high)
    target32 = targets.astype(jnp.float32)
    inner = lax.optimization_barrier(jnp.sum(predicted * target32, axis=1))
    pred_sq = lax.optimization_barrier(jnp.sum(predicted * predicted, axis=1))
    target_sq = lax.optimization_barrier(jnp.sum(target32 * target32, axis=1))
    pred_norm = jnp.sqrt(pred_sq + 1e-06)
    targ_norm = jnp.sqrt(target_sq + 1e-06)
    scale = 1.0 / (pred_norm * targ_norm)
    coef = inner * scale / (pred_norm * pred_norm)
    d_pred = (coef[:, None] * predicted - scale[:, None] * target32).astype(jnp.bfloat16)
    grad = jnp.dot(inputs.T, d_pred.astype(jnp.float32), precision=high)
    moment1 = 0.9 * first_moment + 0.1 * grad
    moment2 = 0.95 * second_moment + 0.05 * grad * grad
    new_map = map_weight - 0.02 * (moment1 / (1.0 - 0.9 ** 10)) / (jnp.sqrt(moment2 / (1.0 - 0.95 ** 10)) + 1e-08)
    joined = jnp.dot(down_weight.astype(jnp.float32), new_map.astype(jnp.bfloat16).astype(jnp.float32), precision=high)
    return (new_map, joined.astype(jnp.bfloat16))
```

```python
import functools

import jax
import jax.numpy as jnp
from jax import lax
from jax.experimental import pallas as pl
from jax.experimental.pallas import tpu as pltpu
from jax.sharding import PartitionSpec as P

BF16 = jnp.bfloat16
F32 = jnp.float32
MESH = pl.DeviceIdType.MESH
VMEM_BYTES = 60 * 1024 * 1024


def place():
    me = lax.axis_index("tok")
    return me // 4, lax.rem(me // 2, 2), lax.rem(me, 2)


def meet(line):
    a, b, c = place()
    barrier = pltpu.get_barrier_semaphore()
    left, right = lax.rem(a + line - 1, line), lax.rem(a + 1, line)
    for t in (
        4 * left + 2 * b + c,
        4 * right + 2 * b + c,
        4 * a + 2 * (1 - b) + c,
        4 * a + 2 * b + 1 - c,
    ):
        pl.semaphore_signal(barrier, inc=1, device_id={"tok": t}, device_id_type=MESH)
    pl.semaphore_wait(barrier, 4)


def remote(src, dst, send, recv, tok):
    return pltpu.make_async_remote_copy(
        src_ref=src, dst_ref=dst, send_sem=send, recv_sem=recv,
        device_id={"tok": tok}, device_id_type=MESH,
    )


def gather_dot_kernel(
    line, lhs_ref, shard_ref, out_ref, held, lhs, acc,
    lhs_sem, own_sem, recv, left_sem, right_sem, y_sem, core_sem,
):
    a, b, c = place()
    depth, width = shard_ref.shape
    tile = min(256, width)

    def slot(x, y, z):
        return 4 * x + 2 * y + z

    def lhs_copy(s):
        columns = pl.ds(pl.multiple_of(s * depth, depth), depth)
        return pltpu.make_async_copy(lhs_ref.at[:, columns], lhs.at[s], lhs_sem.at[s])

    own = pltpu.make_async_copy(shard_ref, held.at[slot(a, b, c)], own_sem)
    own.start()

    @pl.loop(0, 4 * line)
    def _(s):
        lhs_copy(s).start()

    acc[...] = jnp.zeros_like(acc)
    meet(line)
    own.wait()

    def send(s, sem, tok):
        return remote(held.at[s], held.at[s], sem.at[s], recv.at[s], tok)

    def to_left(x):
        return send(slot(x, b, c), left_sem, slot(a - 1, b, c))

    def to_right(x):
        return send(slot(x, b, c), right_sem, slot(a + 1, b, c))

    def to_row(x):
        return send(slot(x, b, c), y_sem, slot(a, 1 - b, c))

    def to_core(x, y):
        return send(slot(x, y, c), core_sem, slot(a, b, 1 - c))

    def arrived(s):
        send(s, core_sem, slot(a, b, 1 - c)).wait_recv()

    def multiply(s):
        lhs_copy(s).wait()

        @pl.loop(0, width // tile)
        def _(n):
            columns = pl.ds(pl.multiple_of(n * tile, tile), tile)
            acc[:, columns] += jnp.dot(
                lhs[s], held[s, :, columns], preferred_element_type=F32
            )

    def each(d, work):
        for sign in (-1, 1):
            x = a + sign * d
            inside = (x >= 0) & (x < line) & (d >= 0) & ((d > 0) | (sign < 0))
            pl.when(inside)(functools.partial(work, x))

    def line_in(x):
        @pl.when(x != a)
        def _():
            arrived(slot(x, b, c))

        @pl.when((x <= a) & (a < line - 1))
        def _():
            to_right(x).start()

        @pl.when((x >= a) & (a > 0))
        def _():
            to_left(x).start()

        to_row(x).start()
        to_core(x, b).start()

    def row_in(x):
        arrived(slot(x, 1 - b, c))
        to_core(x, 1 - b).start()
        multiply(slot(x, 1 - b, c))

    def core_in(y, x):
        arrived(slot(x, y, 1 - c))
        multiply(slot(x, y, 1 - c))

    @pl.loop(0, line + 1)
    def _(d):
        each(d, line_in)
        each(d, lambda x: multiply(slot(x, b, c)))
        each(d - 1, functools.partial(core_in, b))
        each(d - 1, row_in)
        each(d - 2, functools.partial(core_in, 1 - b))

    each(line - 1, functools.partial(core_in, 1 - b))

    @pl.loop(0, line)
    def _(x):
        @pl.when((x <= a) & (a < line - 1))
        def _():
            to_right(x).wait_send()

        @pl.when((x >= a) & (a > 0))
        def _():
            to_left(x).wait_send()

        to_row(x).wait_send()
        to_core(x, b).wait_send()
        to_core(x, 1 - b).wait_send()

    out_ref[...] = acc[...].astype(out_ref.dtype)


def gather_dot(lhs, shard, tok, dtype, collective):
    rows = lhs.shape[0]
    depth, width = shard.shape
    dma = pltpu.SemaphoreType.DMA
    return pl.pallas_call(
        functools.partial(gather_dot_kernel, tok // 4),
        out_shape=jax.ShapeDtypeStruct((rows, width), dtype),
        in_specs=[pl.BlockSpec(memory_space=pl.ANY)] * 2,
        out_specs=pl.BlockSpec(memory_space=pltpu.VMEM),
        scratch_shapes=[
            pltpu.VMEM((tok, depth, width), BF16),
            pltpu.VMEM((tok, rows, depth), BF16),
            pltpu.VMEM((rows, width), F32),
            dma((tok,)), dma, dma((tok,)), dma((tok,)), dma((tok,)), dma((tok,)), dma((tok,)),
        ],
        compiler_params=pltpu.CompilerParams(
            collective_id=collective, has_side_effects=True, vmem_limit_bytes=VMEM_BYTES
        ),
        cost_estimate=pl.CostEstimate(
            flops=2 * rows * width * depth * tok,
            bytes_accessed=2 * rows * depth * tok + 4 * rows * width,
            transcendentals=0,
        ),
    )(lhs, shard)


def dot_scatter_kernel(
    line, act_ref, grad_ref, out_ref,
    core_out, core_in, row_out, row_in, line_out, from_left, from_right,
    core_send, core_recv, row_send, row_recv, line_send, left_recv, right_recv,
):
    a, b, c = place()
    depth, width = out_ref.shape
    tile = min(512, width)
    meet(line)

    def slot(x, y, z):
        return 4 * x + 2 * y + z

    def tiles(work):
        @pl.loop(0, width // tile)
        def _(n):
            work(pl.ds(pl.multiple_of(n * tile, tile), tile))

    def part(s, columns):
        rows = pl.ds(pl.multiple_of(s * depth, depth), depth)
        return lax.dot_general(
            act_ref[:, rows], grad_ref[:, columns], (((0,), (0,)), ((), ())),
            preferred_element_type=F32,
        )

    def core_copy(k):
        return remote(
            core_out.at[k], core_in.at[k], core_send.at[k], core_recv.at[k], slot(a, b, 1 - c)
        )

    def row_copy(x):
        return remote(
            row_out.at[x], row_in.at[x], row_send.at[x], row_recv.at[x], slot(a, 1 - b, c)
        )

    def right_copy(x):
        return remote(
            line_out.at[x], from_left.at[x], line_send.at[x], left_recv.at[x],
            slot(a + 1, b, c),
        )

    def left_copy(x):
        return remote(
            line_out.at[x], from_right.at[x], line_send.at[x], right_recv.at[x],
            slot(a - 1, b, c),
        )

    def each(d, work):
        for sign in (-1, 1):
            x = a + sign * d
            inside = (x >= 0) & (x < line) & (d >= 0) & ((d > 0) | (sign < 0))
            pl.when(inside)(functools.partial(work, x))

    def give_core(y, x):
        k = 2 * x + y

        def work(columns):
            core_out[k, :, columns] = part(slot(x, y, 1 - c), columns).astype(BF16)

        tiles(work)
        core_copy(k).start()

    def give_row(x):
        k = 2 * x + 1 - b
        core_copy(k).wait_recv()

        def work(columns):
            total = part(slot(x, 1 - b, c), columns) + core_in[k, :, columns].astype(F32)
            row_out[x, :, columns] = total.astype(BF16)

        tiles(work)
        row_copy(x).start()

    def total_of(x, columns):
        k = 2 * x + b
        return (
            part(slot(x, b, c), columns)
            + core_in[k, :, columns].astype(F32)
            + row_in[x, :, columns].astype(F32)
        )

    def give_line(x):
        core_copy(2 * x + b).wait_recv()
        row_copy(x).wait_recv()

        def first(columns):
            out_ref[:, columns] = total_of(x, columns)

        tiles(first)

        @pl.when((x >= a) & (a > 0))
        def _():
            right_copy(x).wait_recv()
            tiles(functools.partial(add, from_left, x))

        @pl.when((x <= a) & (a < line - 1))
        def _():
            left_copy(x).wait_recv()
            tiles(functools.partial(add, from_right, x))

        @pl.when(x != a)
        def _():
            def cast(columns):
                line_out[x, :, columns] = out_ref[:, columns].astype(BF16)

            tiles(cast)

        @pl.when(x > a)
        def _():
            right_copy(x).start()

        @pl.when(x < a)
        def _():
            left_copy(x).start()

    def add(ref, x, columns):
        out_ref[:, columns] += ref[x, :, columns].astype(F32)

    @pl.loop(0, line + 1)
    def _(i):
        d = line - 1 - i
        each(d, functools.partial(give_core, 1 - b))
        each(d, give_row)
        each(d, functools.partial(give_core, b))

        @pl.when(i > 0)
        def _():
            each(d + 1, give_line)

    @pl.loop(0, line)
    def _(x):
        core_copy(2 * x).wait_send()
        core_copy(2 * x + 1).wait_send()
        row_copy(x).wait_send()

        @pl.when(x > a)
        def _():
            right_copy(x).wait_send()

        @pl.when(x < a)
        def _():
            left_copy(x).wait_send()


def dot_scatter(activations, d_pred, tok, collective):
    tokens, features = activations.shape
    width = d_pred.shape[1]
    depth = features // tok
    line = tok // 4
    dma = pltpu.SemaphoreType.DMA

    def slots(n):
        return pltpu.VMEM((n, depth, width), BF16)

    return pl.pallas_call(
        functools.partial(dot_scatter_kernel, line),
        out_shape=jax.ShapeDtypeStruct((depth, width), F32),
        in_specs=[pl.BlockSpec(memory_space=pltpu.VMEM)] * 2,
        out_specs=pl.BlockSpec(memory_space=pltpu.VMEM),
        scratch_shapes=[
            slots(2 * line), slots(2 * line), slots(line), slots(line), slots(line),
            slots(line), slots(line),
            dma((2 * line,)), dma((2 * line,)), dma((line,)), dma((line,)), dma((line,)),
            dma((line,)), dma((line,)),
        ],
        compiler_params=pltpu.CompilerParams(
            collective_id=collective, has_side_effects=True, vmem_limit_bytes=VMEM_BYTES
        ),
        cost_estimate=pl.CostEstimate(
            flops=2 * tokens * features * width,
            bytes_accessed=2 * tokens * (features + width),
            transcendentals=0,
        ),
    )(activations, d_pred)


def adam_step(weight, first, second, grad):
    moment1 = 0.9 * first + 0.1 * grad
    moment2 = 0.95 * second + 0.05 * grad * grad
    return weight - 0.02 * (moment1 / (1.0 - 0.9**10)) / (
        jnp.sqrt(moment2 / (1.0 - 0.95**10)) + 1e-08
    )


def per_device(tok, activations, targets, map_weight, first_moment, second_moment, down_weight):
    target32 = targets.astype(F32)
    down_full = lax.all_gather(down_weight, "col", axis=1, tiled=True)
    predicted = gather_dot(activations, map_weight.astype(BF16), tok, F32, 1)
    sums = lax.psum(
        jnp.stack(
            [
                jnp.sum(predicted * target32, axis=1),
                jnp.sum(predicted * predicted, axis=1),
                jnp.sum(target32 * target32, axis=1),
            ]
        ),
        "col",
    )
    inner, pred_sq, target_sq = sums[0], sums[1], sums[2]
    pred_norm = jnp.sqrt(pred_sq + 1e-06)
    targ_norm = jnp.sqrt(target_sq + 1e-06)
    scale = 1.0 / (pred_norm * targ_norm)
    coef = inner * scale / (pred_norm * pred_norm)
    d_pred = (coef[:, None] * predicted - scale[:, None] * target32).astype(BF16)
    grad = dot_scatter(activations, d_pred, tok, 2)
    new_map = adam_step(map_weight, first_moment, second_moment, grad)
    joined = gather_dot(down_full, new_map.astype(BF16), tok, BF16, 3)
    return (new_map, joined)


def solution(mesh):
    split = P("tok", "col")
    return jax.shard_map(
        functools.partial(per_device, mesh.shape["tok"]),
        mesh=mesh,
        in_specs=(P("tok", None),) + (split,) * 5,
        out_specs=(split, split),
        check_vma=False,
    )
```

```python
import functools

import jax
import jax.numpy as jnp
from jax import lax
from jax.experimental import pallas as pl
from jax.experimental.pallas import tpu as pltpu
from jax.sharding import PartitionSpec as P

BF16 = jnp.bfloat16
F32 = jnp.float32
MESH = pl.DeviceIdType.MESH
PIECES = 2
VMEM_BYTES = 60 * 1024 * 1024


def place():
    me = lax.axis_index("tok")
    return me // 4, lax.rem(me // 2, 2), lax.rem(me, 2)


def meet(line):
    a, b, c = place()
    barrier = pltpu.get_barrier_semaphore()
    left, right = lax.rem(a + line - 1, line), lax.rem(a + 1, line)
    for t in (
        4 * left + 2 * b + c,
        4 * right + 2 * b + c,
        4 * a + 2 * (1 - b) + c,
        4 * a + 2 * b + 1 - c,
    ):
        pl.semaphore_signal(barrier, inc=1, device_id={"tok": t}, device_id_type=MESH)
    pl.semaphore_wait(barrier, 4)


def remote(src, dst, send, recv, tok):
    return pltpu.make_async_remote_copy(
        src_ref=src, dst_ref=dst, send_sem=send, recv_sem=recv,
        device_id={"tok": tok}, device_id_type=MESH,
    )


def gather_dot_kernel(
    line, lhs_ref, shard_ref, out_ref, held, lhs, acc,
    lhs_sem, own_sem, recv, left_sem, right_sem, y_sem, core_sem,
):
    a, b, c = place()
    depth, width = shard_ref.shape
    piece = width // PIECES
    tile = min(256, piece)

    def slot(x, y, z):
        return 4 * x + 2 * y + z

    def lhs_copy(s):
        columns = pl.ds(pl.multiple_of(s * depth, depth), depth)
        return pltpu.make_async_copy(lhs_ref.at[:, columns], lhs.at[s], lhs_sem.at[s])

    def own(p):
        columns = pl.ds(p * piece, piece)
        return pltpu.make_async_copy(
            shard_ref.at[:, columns], held.at[slot(a, b, c), p], own_sem.at[p]
        )

    for p in range(PIECES):
        own(p).start()

    @pl.loop(0, 4 * line)
    def _(s):
        lhs_copy(s).start()

    acc[...] = jnp.zeros_like(acc)
    meet(line)
    for p in range(PIECES):
        own(p).wait()

    def send(s, p, sem, tok):
        return remote(held.at[s, p], held.at[s, p], sem.at[s, p], recv.at[s, p], tok)

    def to_left(x, p):
        return send(slot(x, b, c), p, left_sem, slot(a - 1, b, c))

    def to_right(x, p):
        return send(slot(x, b, c), p, right_sem, slot(a + 1, b, c))

    def to_row(x, p):
        return send(slot(x, b, c), p, y_sem, slot(a, 1 - b, c))

    def to_core(x, y, p):
        return send(slot(x, y, c), p, core_sem, slot(a, b, 1 - c))

    def arrived(s, p):
        send(s, p, core_sem, slot(a, b, 1 - c)).wait_recv()

    def multiply(s):
        lhs_copy(s).wait()

        for p in range(PIECES):

            @pl.loop(0, piece // tile)
            def _(n):
                start = pl.multiple_of(n * tile, tile)
                columns = pl.ds(pl.multiple_of(p * piece + start, tile), tile)
                acc[:, columns] += jnp.dot(
                    lhs[s], held[s, p, :, pl.ds(start, tile)], preferred_element_type=F32
                )

    def each(d, work):
        for sign in (-1, 1):
            x = a + sign * d
            inside = (x >= 0) & (x < line) & (d >= 0) & ((d > 0) | (sign < 0))
            pl.when(inside)(functools.partial(work, x))

    def line_in(x):
        for p in range(PIECES):

            @pl.when(x != a)
            def _():
                arrived(slot(x, b, c), p)

            @pl.when((x <= a) & (a < line - 1))
            def _():
                to_right(x, p).start()

            @pl.when((x >= a) & (a > 0))
            def _():
                to_left(x, p).start()

            to_row(x, p).start()
            to_core(x, b, p).start()

    def row_in(x):
        for p in range(PIECES):
            arrived(slot(x, 1 - b, c), p)
            to_core(x, 1 - b, p).start()
        multiply(slot(x, 1 - b, c))

    def core_in(y, x):
        for p in range(PIECES):
            arrived(slot(x, y, 1 - c), p)
        multiply(slot(x, y, 1 - c))

    @pl.loop(0, line + 1)
    def _(d):
        each(d, line_in)
        each(d, lambda x: multiply(slot(x, b, c)))
        each(d - 1, functools.partial(core_in, b))
        each(d - 1, row_in)
        each(d - 2, functools.partial(core_in, 1 - b))

    each(line - 1, functools.partial(core_in, 1 - b))

    @pl.loop(0, line)
    def _(x):
        for p in range(PIECES):

            @pl.when((x <= a) & (a < line - 1))
            def _():
                to_right(x, p).wait_send()

            @pl.when((x >= a) & (a > 0))
            def _():
                to_left(x, p).wait_send()

            to_row(x, p).wait_send()
            to_core(x, b, p).wait_send()
            to_core(x, 1 - b, p).wait_send()

    out_ref[...] = acc[...].astype(out_ref.dtype)


def gather_dot(lhs, shard, tok, dtype, collective):
    rows = lhs.shape[0]
    depth, width = shard.shape
    dma = pltpu.SemaphoreType.DMA
    return pl.pallas_call(
        functools.partial(gather_dot_kernel, tok // 4),
        out_shape=jax.ShapeDtypeStruct((rows, width), dtype),
        in_specs=[pl.BlockSpec(memory_space=pl.ANY)] * 2,
        out_specs=pl.BlockSpec(memory_space=pltpu.VMEM),
        scratch_shapes=[
            pltpu.VMEM((tok, PIECES, depth, width // PIECES), BF16),
            pltpu.VMEM((tok, rows, depth), BF16),
            pltpu.VMEM((rows, width), F32),
            dma((tok,)), dma((PIECES,)),
        ]
        + [dma((tok, PIECES))] * 5,
        compiler_params=pltpu.CompilerParams(
            collective_id=collective, has_side_effects=True, vmem_limit_bytes=VMEM_BYTES
        ),
        cost_estimate=pl.CostEstimate(
            flops=2 * rows * width * depth * tok,
            bytes_accessed=2 * rows * depth * tok + 4 * rows * width,
            transcendentals=0,
        ),
    )(lhs, shard)


def dot_scatter_kernel(
    line, act_ref, grad_ref, out_ref,
    core_out, core_in, row_out, row_in, line_out, from_left, from_right,
    core_send, core_recv, row_send, row_recv, line_send, left_recv, right_recv,
):
    a, b, c = place()
    depth, width = out_ref.shape
    piece = width // PIECES
    tile = min(512, piece)
    meet(line)

    def slot(x, y, z):
        return 4 * x + 2 * y + z

    def tiles(p, work):
        @pl.loop(0, piece // tile)
        def _(n):
            start = pl.multiple_of(n * tile, tile)
            work(pl.ds(start, tile), pl.ds(pl.multiple_of(p * piece + start, tile), tile))

    def part(s, columns):
        rows = pl.ds(pl.multiple_of(s * depth, depth), depth)
        return lax.dot_general(
            act_ref[:, rows], grad_ref[:, columns], (((0,), (0,)), ((), ())),
            preferred_element_type=F32,
        )

    def core_copy(k, p):
        return remote(
            core_out.at[k, p], core_in.at[k, p], core_send.at[k, p], core_recv.at[k, p],
            slot(a, b, 1 - c),
        )

    def row_copy(x, p):
        return remote(
            row_out.at[x, p], row_in.at[x, p], row_send.at[x, p], row_recv.at[x, p],
            slot(a, 1 - b, c),
        )

    def right_copy(x, p):
        return remote(
            line_out.at[x, p], from_left.at[x, p], line_send.at[x, p], left_recv.at[x, p],
            slot(a + 1, b, c),
        )

    def left_copy(x, p):
        return remote(
            line_out.at[x, p], from_right.at[x, p], line_send.at[x, p], right_recv.at[x, p],
            slot(a - 1, b, c),
        )

    def each(d, work):
        for sign in (-1, 1):
            x = a + sign * d
            inside = (x >= 0) & (x < line) & (d >= 0) & ((d > 0) | (sign < 0))
            pl.when(inside)(functools.partial(work, x))

    def give_core(y, x):
        k = 2 * x + y
        for p in range(PIECES):

            def work(inner, columns):
                core_out[k, p, :, inner] = part(slot(x, y, 1 - c), columns).astype(BF16)

            tiles(p, work)
            core_copy(k, p).start()

    def give_row(x):
        k = 2 * x + 1 - b
        for p in range(PIECES):
            core_copy(k, p).wait_recv()

            def work(inner, columns):
                total = part(slot(x, 1 - b, c), columns) + core_in[k, p, :, inner].astype(F32)
                row_out[x, p, :, inner] = total.astype(BF16)

            tiles(p, work)
            row_copy(x, p).start()

    def give_line(x):
        k = 2 * x + b
        for p in range(PIECES):
            core_copy(k, p).wait_recv()

            def local(inner, columns):
                out_ref[:, columns] = (
                    part(slot(x, b, c), columns) + core_in[k, p, :, inner].astype(F32)
                )

            def add(ref, inner, columns):
                out_ref[:, columns] += ref[x, p, :, inner].astype(F32)

            def cast(inner, columns):
                line_out[x, p, :, inner] = out_ref[:, columns].astype(BF16)

            tiles(p, local)
            row_copy(x, p).wait_recv()
            tiles(p, functools.partial(add, row_in))

            @pl.when((x >= a) & (a > 0))
            def _():
                right_copy(x, p).wait_recv()
                tiles(p, functools.partial(add, from_left))

            @pl.when((x <= a) & (a < line - 1))
            def _():
                left_copy(x, p).wait_recv()
                tiles(p, functools.partial(add, from_right))

            @pl.when(x != a)
            def _():
                tiles(p, cast)

            @pl.when(x > a)
            def _():
                right_copy(x, p).start()

            @pl.when(x < a)
            def _():
                left_copy(x, p).start()

    @pl.loop(0, line + 1)
    def _(i):
        d = line - 1 - i
        each(d, functools.partial(give_core, 1 - b))
        each(d, give_row)
        each(d, functools.partial(give_core, b))

        @pl.when(i > 0)
        def _():
            each(d + 1, give_line)

    @pl.loop(0, line)
    def _(x):
        for p in range(PIECES):
            core_copy(2 * x, p).wait_send()
            core_copy(2 * x + 1, p).wait_send()
            row_copy(x, p).wait_send()

            @pl.when(x > a)
            def _():
                right_copy(x, p).wait_send()

            @pl.when(x < a)
            def _():
                left_copy(x, p).wait_send()


def dot_scatter(activations, d_pred, tok, collective):
    tokens, features = activations.shape
    width = d_pred.shape[1]
    depth = features // tok
    line = tok // 4
    dma = pltpu.SemaphoreType.DMA

    def slots(n):
        return pltpu.VMEM((n, PIECES, depth, width // PIECES), BF16)

    return pl.pallas_call(
        functools.partial(dot_scatter_kernel, line),
        out_shape=jax.ShapeDtypeStruct((depth, width), F32),
        in_specs=[pl.BlockSpec(memory_space=pltpu.VMEM)] * 2,
        out_specs=pl.BlockSpec(memory_space=pltpu.VMEM),
        scratch_shapes=[
            slots(2 * line), slots(2 * line), slots(line), slots(line), slots(line),
            slots(line), slots(line),
            dma((2 * line, PIECES)), dma((2 * line, PIECES)),
        ]
        + [dma((line, PIECES))] * 5,
        compiler_params=pltpu.CompilerParams(
            collective_id=collective, has_side_effects=True, vmem_limit_bytes=VMEM_BYTES
        ),
        cost_estimate=pl.CostEstimate(
            flops=2 * tokens * features * width,
            bytes_accessed=2 * tokens * (features + width),
            transcendentals=0,
        ),
    )(activations, d_pred)


def adam_step(weight, first, second, grad):
    moment1 = 0.9 * first + 0.1 * grad
    moment2 = 0.95 * second + 0.05 * grad * grad
    return weight - 0.02 * (moment1 / (1.0 - 0.9**10)) / (
        jnp.sqrt(moment2 / (1.0 - 0.95**10)) + 1e-08
    )


def per_device(tok, col, activations, targets, map_weight, first_moment, second_moment, down_weight):
    target32 = targets.astype(F32)
    down_full = lax.all_gather(down_weight, "col", axis=1, tiled=True)
    predicted = gather_dot(activations, map_weight.astype(BF16), tok, F32, 1)
    own = jnp.stack(
        [
            jnp.sum(predicted * target32, axis=1),
            jnp.sum(predicted * predicted, axis=1),
            jnp.sum(target32 * target32, axis=1),
        ]
    )
    sums = own
    for shift in range(1, col):
        sums += lax.ppermute(own, "col", [(k, (k + shift) % col) for k in range(col)])
    inner, pred_sq, target_sq = sums[0], sums[1], sums[2]
    pred_norm = jnp.sqrt(pred_sq + 1e-06)
    targ_norm = jnp.sqrt(target_sq + 1e-06)
    scale = 1.0 / (pred_norm * targ_norm)
    coef = inner * scale / (pred_norm * pred_norm)
    d_pred = (coef[:, None] * predicted - scale[:, None] * target32).astype(BF16)
    grad = dot_scatter(activations, d_pred, tok, 2)
    new_map = adam_step(map_weight, first_moment, second_moment, grad)
    joined = gather_dot(down_full, new_map.astype(BF16), tok, BF16, 3)
    return (new_map, joined)


def solution(mesh):
    split = P("tok", "col")
    return jax.shard_map(
        functools.partial(per_device, mesh.shape["tok"], mesh.shape["col"]),
        mesh=mesh,
        in_specs=(P("tok", None),) + (split,) * 5,
        out_specs=(split, split),
        check_vma=False,
    )
```
